256 devices in a mesh: dp: 32 (over z_hi, x, y), param: 8 (over z_lo, core).
Axes of the slice: x: 4, y: 4, z: 8 (z_hi: 2, z_lo: 4; z = z_hi * 4 + z_lo), core: 2. Of those that a mesh axis runs over, the one named last changes fastest.
Arguments:
- query_grads: bfloat16 [32, 1280, 1280], P('dp', 'param'), may hold values from -6 to 6
- in_inverse: bfloat16 [1280, 1280], replicated, may hold values from -8.5 to 8.5
- out_inverse: bfloat16 [1280, 1280], replicated, may hold values from -8.5 to 8.5
- activations: bfloat16 [2048, 64, 1280], P('dp', 'param'), may hold values from -6 to 6
- errors: bfloat16 [2048, 64, 1280], P('dp', None, 'param'), may hold values from -6 to 6
Outputs:
- scores: float32 [2048, 32], P(('dp', 'param'))
The draws below stay inside these ranges and needn't reach their ends.
All inputs are finite; a program needn't handle non-finite values.
Results may differ from the reference program's by a relative error of at most 0.0049.
Values may be sent and summed in bfloat16 or wider, within the bound.
A program may use at most 128 MiB of HBM per device.

```python
import math
import jax
import jax.numpy as jnp
from jax import lax

C = 1280
P_SIZE = 64
N = 2048
Q = 32


def inverse_factor(key):
    diag_key, off_key = jax.random.split(key, 2)
    diag_vals = jax.random.uniform(diag_key, (C,), jnp.float32, 1.0, 2.0)
    off_vals = jnp.clip(jax.random.normal(off_key, (C, C), jnp.float32), -4.0, 4.0) * (0.5 / jnp.sqrt(float(C)))
    matrix = off_vals + jnp.eye(C, dtype=jnp.float32) * diag_vals[:, None]
    return matrix


def draw_in_inverse(key, part):
    key = jax.random.fold_in(key, 11)
    return inverse_factor(key).astype(jnp.bfloat16)


def draw_out_inverse(key, part):
    key = jax.random.fold_in(key, 23)
    return inverse_factor(key).astype(jnp.bfloat16)


def block_scale(stream_key, extent, pieces, smallest, top_value):
    loudness, own = 1.0, jax.random.fold_in(stream_key, 6)
    for position, parts in pieces:
        draws = jnp.exp(jax.random.uniform(jax.random.fold_in(own, position), (parts,), jnp.float32, smallest / len(pieces), top_value / len(pieces)))
        loudness = loudness * jnp.repeat(draws, extent[position] // parts).reshape([-1 if axis == position else 1 for axis in range(len(extent))])
    return loudness


def centred(key, extent, spread, limit, cuts=(), held_as=jnp.bfloat16):
    level = block_scale(key, extent, cuts, -0.22, 0.18) if cuts else 1.0
    values = jax.random.normal(key, extent, jnp.float32) * spread * level
    return jnp.minimum(jnp.maximum(values, -limit), limit).astype(held_as)


def setup_inputs(seed: int = 0) -> dict:
    streams_of = jax.random.split(jax.random.key(seed), 6)
    query_grads = centred(streams_of[0], (Q, C, C), 1.0, 6.0, ((0, 32), (1, 8)))
    in_inverse = draw_in_inverse(jax.random.fold_in(streams_of[5], 71), 0)
    out_inverse = draw_out_inverse(jax.random.fold_in(streams_of[5], 71), 0)
    activations = centred(streams_of[3], (N, P_SIZE, C), 1.0, 6.0, ((0, 32), (1, 8)))
    errors = centred(streams_of[4], (N, P_SIZE, C), 1.0, 6.0, ((0, 32), (2, 8)))
    return {"query_grads": query_grads, "in_inverse": in_inverse, "out_inverse": out_inverse, "activations": activations, "errors": errors}


def reference(query_grads, in_inverse, out_inverse, activations, errors):
    mixed_in = jnp.einsum('qoi,ij->qoj', query_grads.astype(jnp.float32), in_inverse.astype(jnp.float32)).astype(jnp.bfloat16)
    preconditioned = jnp.einsum('ko,qoj->qkj', out_inverse.astype(jnp.float32), mixed_in.astype(jnp.float32)).astype(jnp.bfloat16)
    precond_wide = preconditioned.astype(jnp.float32)
    factor = 1.0 / (C * math.sqrt(P_SIZE))
    err_blocks = errors.reshape(N // 16, 16, P_SIZE, C)
    act_blocks = activations.reshape(N // 16, 16, P_SIZE, C)

    def score_block(pair):
        err_part, act_part = pair
        example_grad = jnp.einsum('npo,npi->noi', err_part.astype(jnp.float32), act_part.astype(jnp.float32)).astype(jnp.bfloat16)
        return jnp.einsum('noi,qoi->nq', example_grad.astype(jnp.float32), precond_wide) * factor
    result = lax.map(score_block, (err_blocks, act_blocks))
    return result.reshape(N, Q)
```

```python
import math

import jax
import jax.numpy as jnp
from jax import lax
from jax.experimental import pallas as pl
from jax.experimental.pallas import tpu as pltpu
from jax.sharding import PartitionSpec as P

MESH = pl.DeviceIdType.MESH
BF16 = jnp.bfloat16
F32 = jnp.float32
QUADS = 16
UNITS = 10
HALF = 640
WIDE = 4 * HALF


def dot(a, b, dims):
    return lax.dot_general(a, b, (dims, ((), ())), preferred_element_type=F32)


def kernel(
    g_in, iinv_in, oinv_in, a_in, e_in, out,
    g, iv, ob, mstage, mbuf, w, abuf, ebuf, eg, acc, part, rbuf,
    lsem, dsem, msend, mrecv, xsend, xrecv, asend, arecv, fsend, frecv,
):
    dp, pa = lax.axis_index("dp"), lax.axis_index("param")
    zh, x, y = dp // 16, (dp // 4) % 4, dp % 4
    zl, c = pa // 2, pa % 2
    z = zh * 4 + zl
    o = 1 - c
    slot = x * 4 + y

    def at_z(k):
        t = (z + k + 8) % 8
        return ((t // 4) * 16 + slot, (t % 4) * 2 + c)

    def at_xy(dx, dy):
        return (zh * 16 + ((x + dx + 4) % 4) * 4 + (y + dy + 4) % 4, pa)

    partner = (dp, zl * 2 + o)

    def remote(src, dst, ssem, rsem, dev):
        return pltpu.make_async_remote_copy(src, dst, ssem, rsem, device_id=dev, device_id_type=MESH)

    def half_at(ref, h):
        return ref.at[:, :, pl.ds(pl.multiple_of(h * HALF, 128), HALF)]

    loads = [
        pltpu.make_async_copy(g_in, g, lsem.at[0]),
        pltpu.make_async_copy(iinv_in.at[:, pl.ds(pl.multiple_of(o * HALF, 128), HALF)], iv.at[1], lsem.at[1]),
        pltpu.make_async_copy(iinv_in.at[:, pl.ds(pl.multiple_of(c * HALF, 128), HALF)], iv.at[0], lsem.at[2]),
        pltpu.make_async_copy(oinv_in.at[pl.ds(pl.multiple_of(zl * 320, 64), 320)], ob, lsem.at[3]),
        pltpu.make_async_copy(half_at(a_in, c), abuf.at[:, zl, c], lsem.at[4]),
        pltpu.make_async_copy(e_in, ebuf.at[c], lsem.at[5]),
    ]
    for cp in loads:
        cp.start()

    barrier = pltpu.get_barrier_semaphore()
    for dev in (at_z(1), at_z(-1), at_xy(1, 0), at_xy(-1, 0), at_xy(0, 1), at_xy(0, -1)):
        pl.semaphore_signal(barrier, inc=1, device_id=dev, device_id_type=MESH)
    for j in range(1, 8):
        pl.semaphore_signal(barrier, inc=1, device_id=(dp, (pa + j) % 8), device_id_type=MESH)
    pl.semaphore_wait(barrier, 13)

    loads[0].wait()
    loads[1].wait()
    mstage[...] = dot(g[...], iv[1], ((1,), (0,))).astype(BF16)
    swap_m = remote(mstage, mbuf.at[z, c], dsem.at[0], dsem.at[1], partner)
    swap_m.start()
    loads[2].wait()
    mbuf[z, c] = dot(g[...], iv[0], ((1,), (0,))).astype(BF16)

    def m_copy(d, j, i):
        block = (z - d * j + 8) % 8
        which = c if i == 0 else o
        ref = mbuf.at[block, which]
        k = 0 if d > 0 else 1
        return remote(ref, ref, msend.at[k, j, i], mrecv.at[k, j, i], at_z(d))

    sent_m = []
    swap_a = remote(half_at(a_in, o), abuf.at[:, zl, c], dsem.at[2], dsem.at[3], partner)
    swap_e = remote(e_in, ebuf.at[c], dsem.at[4], dsem.at[5], partner)
    for j in range(4):
        for i in range(2):
            if j == 0 and i == 1:
                swap_m.wait_recv()
            for k, d in enumerate((1, -1)):
                if j > 0:
                    m_copy(d, j - 1, i).wait_recv()
                if j < 3 or i == k:
                    cp = m_copy(d, j, i)
                    cp.start()
                    sent_m.append(cp)
        if j == 0:
            swap_a.start()
            swap_e.start()
            for cp in loads[3:]:
                cp.wait()
    swap_a.wait_recv()

    def a_copy(d, j, k):
        block = (zl - d * j + 8) % 4
        ref = abuf.at[k, block]
        i = 0 if d > 0 else 1
        return remote(ref, ref, asend, arecv.at[i, j, k], at_z(d))

    def a_step(j, k):
        for d in (1, -1):
            there = (zl >= j) if d > 0 else (zl <= 3 - j)
            more = (zl < 3) if d > 0 else (zl > 0)

            @pl.when(there & (k >= 0) & (k < QUADS))
            def _():
                if j > 0:
                    a_copy(d, j - 1, k).wait_recv()
                if j < 3:

                    @pl.when(more)
                    def _():
                        a_copy(d, j, k).start()

    a_step(0, jnp.int32(0))
    a_step(0, jnp.int32(1))
    m_copy(1, 3, 0).wait_recv()
    m_copy(-1, 3, 1).wait_recv()

    p0 = dot(ob[...], mbuf[0:4].reshape(1280, HALF), ((1,), (0,))).reshape(40, 8, HALF)
    p1 = dot(ob[...], mbuf[4:8].reshape(1280, HALF), ((1,), (0,))).reshape(40, 8, HALF)
    p = jnp.concatenate([p0, p1], axis=1).astype(BF16).reshape(UNITS, 4, 16, HALF)
    for k in range(4):
        w[:, slot, :, k * HALF : (k + 1) * HALF] = p[:, k]

    def place(first, d1, d2):
        dx, dy = (d1, d2) if first == 0 else (d2, d1)
        return ((x + dx + 4) % 4) * 4 + (y + dy + 4) % 4

    def neighbour(first, axis, d):
        return at_xy(d, 0) if (first == axis) else at_xy(0, d)

    def x_copy(v, first, axis, d, d1, whole):
        u = 2 * v + first
        k = 0 if d > 0 else 1
        if axis == 0:
            s = place(first, 0 if whole else -d, 0)
            sem = k if whole else 2 + k
        else:
            s = place(first, d1, 0 if whole else -d)
            sem = 4 + (d1 + 1) * 4 + (k if whole else 2 + k)
        ref = w.at[u, s]
        if not whole:
            ref = ref.at[:, pl.ds(k * 2 * HALF, 2 * HALF)]
        return remote(ref, ref, xsend.at[u], xrecv.at[u, sem], neighbour(first, axis, d))

    both = (1, -1)

    def stage0(v):
        for d in both:
            for first in (0, 1):
                x_copy(v, first, 0, d, 0, True).start()
        for d in both:
            for first in (0, 1):
                x_copy(v, first, 1, d, 0, True).start()

    def stage1(v):
        for d in both:
            for first in (0, 1):
                x_copy(v, first, 0, d, 0, True).wait_recv()
                x_copy(v, first, 0, d, 0, False).start()
                for e in both:
                    x_copy(v, first, 1, e, -d, True).start()
        for d in both:
            for first in (0, 1):
                x_copy(v, first, 1, d, 0, True).wait_recv()
                x_copy(v, first, 1, d, 0, False).start()

    def stage2(v):
        for first in (0, 1):
            for d in both:
                x_copy(v, first, 0, d, 0, False).wait_recv()
            for e in both:
                x_copy(v, first, 1, e, 2, True).start()
        for d1 in both:
            for d in both:
                for first in (0, 1):
                    x_copy(v, first, 1, d, d1, True).wait_recv()
                    x_copy(v, first, 1, d, d1, False).start()

    def stage3(v):
        for d in both:
            for first in (0, 1):
                x_copy(v, first, 1, d, 2, True).wait_recv()
                x_copy(v, first, 1, d, 2, False).start()

    def stage4(v):
        for d1 in (0, 1, -1, 2):
            for d in both:
                for first in (0, 1):
                    x_copy(v, first, 1, d, d1, False).wait_recv()

    def example_grads(k):
        a4 = abuf[k].astype(F32).reshape(8, 4, 8, HALF)
        for pair in range(2):
            acts = [a4[:, 2 * pair + i].reshape(64, HALF).astype(BF16) for i in range(2)]
            for cc in range(2):
                grads = [
                    dot(ebuf[cc, k * 4 + 2 * pair + i], acts[i], ((0,), (0,))).reshape(20, 8, HALF)
                    for i in range(2)
                ]
                both_images = jnp.concatenate(grads, axis=1).astype(BF16).reshape(5, 4, 16, HALF)
                for j in range(4):
                    eg[5 * cc : 5 * cc + 5, k * 2 + pair, :, j * HALF : (j + 1) * HALF] = both_images[:, j]

    swap_e.wait_recv()

    def step(t, carry):
        v = t // 3

        @pl.when((t % 3 == 0) & (v < 5))
        def _():
            stage0(v)

        a_step(0, t + 2)

        @pl.when((t % 3 == 0) & (v >= 1) & (v <= 5))
        def _():
            stage3(v - 1)

        @pl.when((t % 3 == 1) & (v < 5))
        def _():
            stage1(v)

        @pl.when((t % 3 == 1) & (v >= 1) & (v <= 5))
        def _():
            stage4(v - 1)

        @pl.when((t % 3 == 2) & (v < 5))
        def _():
            stage2(v)

        a_step(1, t)
        a_step(2, t - 1)
        a_step(3, t - 2)

        @pl.when((t >= 2) & (t < QUADS + 2))
        def _():
            example_grads(t - 2)

        return carry

    lax.fori_loop(0, QUADS + 2, step, 0)

    acc[...] = jnp.zeros_like(acc)

    def score(u, carry):
        acc[...] += dot(eg[u].reshape(512, WIDE), w[u].reshape(256, WIDE), ((1,), (1,)))
        return carry

    lax.fori_loop(0, UNITS, score, 0)
    row = lax.broadcasted_iota(jnp.int32, (512, 256), 0)
    col = lax.broadcasted_iota(jnp.int32, (512, 256), 1)
    sums = jnp.where(row % 8 == col % 8, acc[...], 0.0).reshape(64, 8, 256).sum(axis=1)
    col = lax.broadcasted_iota(jnp.int32, (256, 128), 0)
    query = lax.broadcasted_iota(jnp.int32, (256, 128), 1)
    pick = jnp.where(((col // 8) % 2) * 16 + col // 16 == query, 1.0, 0.0).astype(F32)
    part[...] = jnp.dot(sums, pick, preferred_element_type=F32, precision=lax.Precision.HIGHEST)

    shares = []
    for j in range(1, 8):
        to = (pa + j) % 8
        cp = remote(part.at[pl.ds(pl.multiple_of(to * 8, 8), 8)], rbuf.at[j - 1], fsend.at[j - 1], frecv.at[j - 1], (dp, to))
        cp.start()
        shares.append(cp)
    total = part[pl.ds(pl.multiple_of(pa * 8, 8), 8)]
    for j in range(7):
        shares[j].wait_recv()
        total = total + rbuf[j]
    out[...] = total[:, :32] * (1.0 / (1280 * math.sqrt(64)))

    for cp in shares + sent_m + [swap_m, swap_a, swap_e]:
        cp.wait_send()

    def all_sent(u, carry):
        ref = w.at[u, pl.ds(0, 15)]
        remote(ref, ref, xsend.at[u], xrecv.at[u, 0], partner).wait_send()
        return carry

    lax.fori_loop(0, UNITS, all_sent, 0)
    inner = (zl == 1) | (zl == 2)

    @pl.when(inner)
    def _():
        ref = w.at[pl.ds(0, 5)]
        remote(ref, ref, asend, xrecv.at[0, 0], partner).wait_send()

    @pl.when(jnp.logical_not(inner))
    def _():
        ref = w.at[0]
        remote(ref, ref, asend, xrecv.at[0, 0], partner).wait_send()


def per_device(query_grads, in_inverse, out_inverse, activations, errors):
    dma = pltpu.SemaphoreType.DMA
    return pl.pallas_call(
        kernel,
        out_shape=jax.ShapeDtypeStruct((8, 32), F32),
        in_specs=[pl.BlockSpec(memory_space=pl.ANY)] * 5,
        out_specs=pl.BlockSpec(memory_space=pltpu.VMEM),
        scratch_shapes=[
            pltpu.VMEM((160, 1280), BF16),
            pltpu.VMEM((2, 1280, HALF), BF16),
            pltpu.VMEM((320, 1280), BF16),
            pltpu.VMEM((160, HALF), BF16),
            pltpu.VMEM((8, 2, 160, HALF), BF16),
            pltpu.VMEM((UNITS, 16, 16, WIDE), BF16),
            pltpu.VMEM((QUADS, 4, 2, 32, HALF), BF16),
            pltpu.VMEM((2, 64, 64, 160), BF16),
            pltpu.VMEM((UNITS, 32, 16, WIDE), BF16),
            pltpu.VMEM((512, 256), F32),
            pltpu.VMEM((64, 128), F32),
            pltpu.VMEM((7, 8, 128), F32),
            dma((6,)),
            dma((6,)),
            dma((2, 4, 2)),
            dma((2, 4, 2)),
            dma((UNITS,)),
            dma((UNITS, 20)),
            dma,
            dma((2, 3, QUADS)),
            dma((7,)),
            dma((7,)),
        ],
        compiler_params=pltpu.CompilerParams(
            collective_id=0, has_side_effects=True, vmem_limit_bytes=63 * 1024 * 1024
        ),
        cost_estimate=pl.CostEstimate(flops=4 * 10**9, bytes_accessed=10**7, transcendentals=0),
    )(
        query_grads.reshape(160, 1280),
        in_inverse,
        out_inverse,
        activations.reshape(QUADS, 32, 1280),
        errors,
    )


def solution(mesh):
    return jax.shard_map(
        per_device,
        mesh=mesh,
        in_specs=(P("dp", "param", None), P(), P(), P("dp", "param", None), P("dp", None, "param")),
        out_specs=P(("dp", "param"), None),
        check_vma=False,
    )
```

```python
import math

import jax
import jax.numpy as jnp
from jax import lax
from jax.experimental import pallas as pl
from jax.experimental.pallas import tpu as pltpu
from jax.sharding import PartitionSpec as P

MESH = pl.DeviceIdType.MESH
BF16 = jnp.bfloat16
F32 = jnp.float32
GROUPS = 8
AHEAD = 2
LAG = 3
LAST = 24
UNITS = 10
HALF = 640
WIDE = 20 * 128
CUTS = ((0, 384), (384, 640))
EARLY = 384


def dot(a, b, dims):
    return lax.dot_general(a, b, (dims, ((), ())), preferred_element_type=F32)


def kernel(
    g_in, iinv_in, oinv_in, a_in, e_in, out,
    g, iv, ob, mstage0, mstage1, mbuf0, mbuf1, w, abuf, ebuf, et, eg, acc, part, rbuf,
    lsem, msend, mrecv, mdsend, mdrecv, esend, erecv, xsend, xrecv, asend, arecv, adsend, adrecv, fsend, frecv,
):
    dp, pa = lax.axis_index("dp"), lax.axis_index("param")
    zh, x, y = dp // 16, (dp // 4) % 4, dp % 4
    zl, c = pa // 2, pa % 2
    z = zh * 4 + zl
    h = zl % 2
    near = zl + 1 - 2 * h
    slot = x * 4 + y

    def at_z(k):
        t = (z + k + 8) % 8
        return ((t // 4) * 16 + slot, (t % 4) * 2 + c)

    def at_xy(dx, dy):
        return (zh * 16 + ((x + dx + 4) % 4) * 4 + (y + dy + 4) % 4, pa)

    partner = (dp, zl * 2 + 1 - c)

    def remote(src, dst, ssem, rsem, dev):
        return pltpu.make_async_remote_copy(src, dst, ssem, rsem, device_id=dev, device_id_type=MESH)

    def lanes(half):
        return pl.ds(pl.multiple_of(half * HALF, 128), HALF)

    loads = [
        pltpu.make_async_copy(g_in, g, lsem.at[0]),
        pltpu.make_async_copy(iinv_in.at[:, lanes(1 - h)], iv.at[1], lsem.at[1]),
        pltpu.make_async_copy(iinv_in.at[:, lanes(h)], iv.at[0], lsem.at[2]),
        pltpu.make_async_copy(e_in, ebuf, lsem.at[3]),
        pltpu.make_async_copy(a_in.at[:, :, :, lanes(h)], abuf.at[:, zl, c], lsem.at[4]),
    ] + [
        pltpu.make_async_copy(
            oinv_in.at[pl.ds(pl.multiple_of((zl - h + k) * 320 + c * 160, 32), 160)], ob.at[pl.ds(k * 160, 160)], lsem.at[5 + k]
        )
        for k in (0, 1)
    ]
    for cp in loads:
        cp.start()

    barrier = pltpu.get_barrier_semaphore()
    for dev in (at_z(1), at_z(-1), at_z(2), at_z(-2), at_xy(1, 0), at_xy(-1, 0), at_xy(0, 1), at_xy(0, -1)):
        pl.semaphore_signal(barrier, inc=1, device_id=dev, device_id_type=MESH)
    for j in range(1, 8):
        pl.semaphore_signal(barrier, inc=1, device_id=(dp, (pa + j) % 8), device_id_type=MESH)
    pl.semaphore_wait(barrier, 15)

    mstage, mbuf = (mstage0, mstage1), (mbuf0, mbuf1)

    def m_copy(n, d, kind):
        k = (0 if d > 0 else 4) + kind
        if kind == 0:
            return remote(mstage[n], mbuf[n].at[z, c], msend.at[n, k], mrecv.at[n, k], at_z(d))
        ref = mbuf[n].at[(z - d * (kind - 1) + 8) % 8, c]
        if kind == 3:
            ref = ref.at[pl.ds(0 if d > 0 else 80, 80)]
        return remote(ref, ref, msend.at[n, k], mrecv.at[n, k], at_z(2 * d))

    def m_share(n, j, k):
        ref = mbuf[n].at[(z + j + 8) % 8, c]
        return remote(ref, ref, mdsend.at[n, k], mdrecv.at[n, k], partner)

    both = (1, -1)
    sent = []

    def send(cp):
        cp.start()
        sent.append(cp)

    def m_other(n):
        lo, hi = CUTS[n]
        mstage[n][...] = dot(g[...], iv[1, :, lo:hi], ((1,), (0,))).astype(BF16)

    def m_own(n):
        lo, hi = CUTS[n]
        mbuf[n][z, c] = dot(g[...], iv[0, :, lo:hi], ((1,), (0,))).astype(BF16)

    def m_first(n):
        for i, d in enumerate(both):
            m_copy(n, d, 0).wait_recv()
            send(m_copy(n, d, 2))
            send(m_share(n, -d, 1 + i))

    def m_second(n):
        for i, d in enumerate(both):
            m_copy(n, d, 1).wait_recv()
            send(m_copy(n, d, 3))
            send(m_share(n, -2 * d, 3 + i))

    def m_last(n):
        for i, d in enumerate(both):
            m_copy(n, d, 2).wait_recv()
            send(m_share(n, -3 * d, 5 + i))
        for d in both:
            m_copy(n, d, 3).wait_recv()
        send(m_share(n, 4, 7))
        for k, j in enumerate((0, -1, 1, -2, 2, -3, 3, 4)):
            m_share(n, j, k).wait_recv()

    def turn(i, carry):
        et[h, i] = ebuf[pl.ds(2 * i, 2)].reshape(128, 160).T
        return carry

    loads[0].wait()
    loads[1].wait()
    m_other(0)
    for d in both:
        send(m_copy(0, d, 0))
    loads[2].wait()
    m_own(0)
    for d in both:
        send(m_copy(0, d, 1))
    send(m_share(0, 0, 0))
    m_other(1)
    m_own(1)
    m_first(0)
    m_second(0)
    for kind in (0, 1):
        for d in both:
            send(m_copy(1, d, kind))
    send(m_share(1, 0, 0))
    loads[3].wait()
    lax.fori_loop(0, 32, turn, 0)
    loads[4].wait()

    def e_copy(k):
        ref = et.at[h, pl.ds(k * 4, 4)]
        return remote(ref, ref, esend, erecv.at[k], (dp, near * 2 + c))

    def a_send(k):
        @pl.when(k < GROUPS)
        def _():
            e_copy(k).start()
            for d in both:

                @pl.when((zl + d >= 0) & (zl + d <= 3))
                def _():
                    a_copy(k, zl, a_in.at[k, :, :, lanes(1 - h)], d).start()

            for d in both:

                @pl.when((zl + 2 * d >= 0) & (zl + 2 * d <= 3))
                def _():
                    a_copy(k, zl, abuf.at[k, zl, c], 2 * d).start()

    def a_copy(k, block, src, d):
        return remote(src, abuf.at[k, block, c], asend, arecv.at[block, k], at_z(d))

    def a_share(k, block):
        ref = abuf.at[k, block, c]
        return remote(ref, ref, adsend, adrecv.at[block, k], partner)

    def middle(block):
        return ((zl == 1) & (block == 0)) | ((zl == 2) & (block == 3))

    def a_pass(k):
        for block in (0, 3):

            @pl.when(middle(block))
            def _():
                ref = abuf.at[k, block, c]
                a_copy(k, block, ref, 1).wait_recv()
                a_copy(k, block, ref, 2 if block == 0 else -2).start()
                a_share(k, block).start()

    def a_collect(k):
        for j in range(1, 4):
            block = (zl + j) % 4

            @pl.when(jnp.logical_not(middle(block)))
            def _():
                a_copy(k, block, abuf.at[k, block, c], 1).wait_recv()
                a_share(k, block).start()

    def a_ready(k):
        for j in range(4):
            a_share(k, (zl + j) % 4).wait_recv()
        e_copy(k).wait_recv()

    def place(first, d1, d2):
        dx, dy = (d1, d2) if first == 0 else (d2, d1)
        return ((x + dx + 4) % 4) * 4 + (y + dy + 4) % 4

    def neighbour(first, axis, d):
        return at_xy(d, 0) if (first == axis) else at_xy(0, d)

    def x_copy(v, first, axis, d, d1, whole):
        u = 2 * v + first
        k = 0 if d > 0 else 1
        if axis == 0:
            s = place(first, 0 if whole else -d, 0)
            sem = k if whole else 2 + k
        else:
            s = place(first, d1, 0 if whole else -d)
            sem = 4 + (d1 + 1) * 4 + (k if whole else 2 + k)
        ref = w.at[u, s]
        if not whole:
            ref = ref.at[:, pl.ds(k * 2 * HALF, 2 * HALF)]
        return remote(ref, ref, xsend.at[u], xrecv.at[u, sem], neighbour(first, axis, d))

    def stage0(v):
        for d in both:
            for first in (0, 1):
                x_copy(v, first, 0, d, 0, True).start()
        for d in both:
            for first in (0, 1):
                x_copy(v, first, 1, d, 0, True).start()

    def stage1(v):
        for d in both:
            for first in (0, 1):
                x_copy(v, first, 0, d, 0, True).wait_recv()
                x_copy(v, first, 0, d, 0, False).start()
                for e in both:
                    x_copy(v, first, 1, e, -d, True).start()
        for d in both:
            for first in (0, 1):
                x_copy(v, first, 1, d, 0, True).wait_recv()
                x_copy(v, first, 1, d, 0, False).start()

    def stage2(v):
        for first in (0, 1):
            for d in both:
                x_copy(v, first, 0, d, 0, False).wait_recv()
            for e in both:
                x_copy(v, first, 1, e, 2, True).start()
        for d1 in both:
            for d in both:
                for first in (0, 1):
                    x_copy(v, first, 1, d, d1, True).wait_recv()
                    x_copy(v, first, 1, d, d1, False).start()

    def stage3(v):
        for d in both:
            for first in (0, 1):
                x_copy(v, first, 1, d, 2, True).wait_recv()
                x_copy(v, first, 1, d, 2, False).start()

    def stage4(v):
        for d1 in (0, 1, -1, 2):
            for d in both:
                for first in (0, 1):
                    x_copy(v, first, 1, d, d1, False).wait_recv()

    def precondition(n):
        lo, hi = CUTS[n]
        p = [
            dot(ob[...], mbuf[n][4 * k : 4 * k + 4].reshape(1280, hi - lo), ((1,), (0,))).reshape(40, 8, hi - lo)
            for k in (0, 1)
        ]
        p = jnp.concatenate(p, axis=1).astype(BF16)
        for i in range(lo // 128, hi // 128):
            for k in range(40):
                u, place_in = 2 * i + k // 20, 128 * (k % 20)
                w[u, slot, :, place_in : place_in + 128] = p[k, :, 128 * i - lo : 128 * i - lo + 128]

    for k in range(GROUPS):
        a_share(k, zl).start()
    loads[5].wait()
    loads[6].wait()
    m_last(0)
    precondition(0)
    for v in range(3):
        stage0(v)
    m_first(1)
    m_second(1)
    a_send(jnp.int32(0))
    stage1(0)
    m_last(1)
    for k in range(1, AHEAD):
        a_send(jnp.int32(k))
    precondition(1)
    acc[...] = jnp.zeros_like(acc)

    left_half = lax.broadcasted_iota(jnp.int32, (160, 128), 1) < 64

    def example_grads(k):
        a8 = abuf[k].astype(F32).reshape(8, 2, 4, 8, HALF)
        for pair in range(4):
            quad, i = pair // 2, 2 * (pair % 2)
            acts = jnp.concatenate([a8[:, quad, i].reshape(64, HALF), a8[:, quad, i + 1].reshape(64, HALF)], axis=0).astype(BF16)
            for cc in range(2):
                errs = et[cc, k * 4 + pair].astype(F32)
                pieces = [
                    dot(jnp.where(left_half, errs, 0.0).astype(BF16), acts, ((1,), (0,))).reshape(20, 8, HALF),
                    dot(jnp.where(left_half, 0.0, errs).astype(BF16), acts, ((1,), (0,))).reshape(20, 8, HALF),
                ]
                both_images = jnp.concatenate(pieces, axis=1).astype(BF16)
                for i in range(5):
                    for j in range(20):
                        eg[2 * i + cc, k * 4 + pair, :, j * 128 : j * 128 + 128] = both_images[j, :, i * 128 : i * 128 + 128]

    def score(v, lo, hi):
        total = acc[lo:hi]
        for u in (2 * v, 2 * v + 1):
            total += dot(eg[u, lo // 16 : hi // 16].reshape(hi - lo, WIDE), w[u].reshape(256, WIDE), ((1,), (1,)))
        acc[lo:hi] = total

    def step(t, carry):
        v = t // 3

        @pl.when((t % 3 == 0) & (v >= 1) & (v < 5))
        def _():
            stage1(v)

        @pl.when((t % 3 == 0) & (v < 2))
        def _():
            stage0(v + 3)

        @pl.when((t % 3 == 1) & (v >= 1) & (v <= 5))
        def _():
            stage2(v - 1)

        @pl.when((t % 3 == 2) & (v >= 2) & (v <= 6))
        def _():
            stage3(v - 2)

        k = t // 2

        @pl.when((t % 2 == 0) & (k < GROUPS))
        def _():
            a_pass(k)
            a_send(k + AHEAD)

        @pl.when((t % 2 == 1) & (k >= LAG) & (k < GROUPS + LAG))
        def _():
            a_collect(k - LAG)

        @pl.when((t % 2 == 0) & (k >= LAG + 1) & (k < GROUPS + LAG + 1))
        def _():
            a_ready(k - LAG - 1)
            example_grads(k - LAG - 1)

        @pl.when((t % 3 == 2) & (v >= 3) & (v <= 7))
        def _():
            stage4(v - 3)

        @pl.when((t >= LAST - 5) & (t < LAST))
        def _():
            score(t - LAST + 5, 0, EARLY)

        return carry

    lax.fori_loop(0, LAST, step, 0)

    def score_late(v, carry):
        score(v, EARLY, 512)
        return carry

    lax.fori_loop(0, 5, score_late, 0)

    row = lax.broadcasted_iota(jnp.int32, (512, 256), 0)
    col = lax.broadcasted_iota(jnp.int32, (512, 256), 1)
    sums = jnp.where(row % 8 == col % 8, acc[...], 0.0).reshape(64, 8, 256).sum(axis=1)
    col = lax.broadcasted_iota(jnp.int32, (256, 128), 0)
    query = lax.broadcasted_iota(jnp.int32, (256, 128), 1)
    pick = jnp.where(((col // 8) % 2) * 16 + col // 16 == query, 1.0, 0.0).astype(F32)
    part[...] = jnp.dot(sums, pick, preferred_element_type=F32, precision=lax.Precision.HIGHEST)

    shares = []
    for j in range(1, 8):
        to = (pa + j) % 8
        cp = remote(part.at[pl.ds(pl.multiple_of(to * 8, 8), 8)], rbuf.at[j - 1], fsend.at[j - 1], frecv.at[j - 1], (dp, to))
        cp.start()
        shares.append(cp)
    total = part[pl.ds(pl.multiple_of(pa * 8, 8), 8)]
    for j in range(7):
        shares[j].wait_recv()
        total = total + rbuf[j]
    out[...] = total[:, :32] * (1.0 / (1280 * math.sqrt(64)))

    for cp in shares + sent:
        cp.wait_send()

    def all_sent(u, carry):
        ref = w.at[u, pl.ds(0, 15)]
        remote(ref, ref, xsend.at[u], xrecv.at[u, 0], partner).wait_send()
        return carry

    lax.fori_loop(0, UNITS, all_sent, 0)
    remote(et.at[0], et.at[0], esend, erecv.at[0], partner).wait_send()
    ref = abuf.at[:, :, 0]
    remote(ref, ref, adsend, arecv.at[0, 0], partner).wait_send()
    inner = (zl == 1) | (zl == 2)

    @pl.when(inner)
    def _():
        ref = abuf.at[:, :, 0]
        remote(ref, ref, asend, arecv.at[0, 0], partner).wait_send()

    @pl.when(jnp.logical_not(inner))
    def _():
        ref = abuf.at[:, pl.ds(0, 2), 0]
        remote(ref, ref, asend, arecv.at[0, 0], partner).wait_send()


def per_device(query_grads, in_inverse, out_inverse, activations, errors):
    dma = pltpu.SemaphoreType.DMA
    return pl.pallas_call(
        kernel,
        out_shape=jax.ShapeDtypeStruct((8, 32), F32),
        in_specs=[pl.BlockSpec(memory_space=pl.ANY)] * 5,
        out_specs=pl.BlockSpec(memory_space=pltpu.VMEM),
        scratch_shapes=[
            pltpu.VMEM((160, 1280), BF16),
            pltpu.VMEM((2, 1280, HALF), BF16),
            pltpu.VMEM((320, 1280), BF16),
            pltpu.VMEM((160, 384), BF16),
            pltpu.VMEM((160, 256), BF16),
            pltpu.VMEM((8, 2, 160, 384), BF16),
            pltpu.VMEM((8, 2, 160, 256), BF16),
            pltpu.VMEM((UNITS, 16, 16, WIDE), BF16),
            pltpu.VMEM((GROUPS, 4, 2, 2, 32, HALF), BF16),
            pltpu.VMEM((64, 64, 160), BF16),
            pltpu.VMEM((2, 32, 160, 128), BF16),
            pltpu.VMEM((UNITS, 32, 16, WIDE), BF16),
            pltpu.VMEM((512, 256), F32),
            pltpu.VMEM((64, 128), F32),
            pltpu.VMEM((7, 8, 128), F32),
            dma((7,)),
            dma((2, 8)),
            dma((2, 8)),
            dma((2, 8)),
            dma((2, 8)),
            dma,
            dma((GROUPS,)),
            dma((UNITS,)),
            dma((UNITS, 20)),
            dma,
            dma((4, GROUPS)),
            dma,
            dma((4, GROUPS)),
            dma((7,)),
            dma((7,)),
        ],
        compiler_params=pltpu.CompilerParams(
            collective_id=0, has_side_effects=True, vmem_limit_bytes=63 * 1024 * 1024
        ),
        cost_estimate=pl.CostEstimate(flops=4 * 10**9, bytes_accessed=10**7, transcendentals=0),
    )(
        query_grads.reshape(160, 1280),
        in_inverse,
        out_inverse,
        activations.reshape(GROUPS, 2, 32, 1280),
        errors,
    )


def solution(mesh):
    return jax.shard_map(
        per_device,
        mesh=mesh,
        in_specs=(P("dp", "param", None), P(), P(), P("dp", "param", None), P("dp", None, "param")),
        out_specs=P(("dp", "param"), None),
        check_vma=False,
    )
```

```python
import math

import jax
import jax.numpy as jnp
from jax import lax
from jax.experimental import pallas as pl
from jax.experimental.pallas import tpu as pltpu
from jax.sharding import PartitionSpec as P

MESH = pl.DeviceIdType.MESH
BF16 = jnp.bfloat16
F32 = jnp.float32
GROUPS = 8
STEPS = 27
LATE = 256
UNITS = 10
HALF = 640
WIDE = 20 * 128
CUTS = ((0, 128), (128, 384), (384, 640))


def dot(a, b, dims):
    return lax.dot_general(a, b, (dims, ((), ())), preferred_element_type=F32)


def kernel(
    g_in, iinv_in, oinv_in, a_in, e_in, out,
    g, iv, ob, mstage0, mstage1, mstage2, mbuf0, mbuf1, mbuf2, w, abuf, ebuf, et, eg, acc, part, rbuf,
    lsem, msend, mrecv, mdsend, mdrecv, esend, erecv, xsend, xrecv, asend, arecv, adsend, adrecv, fsend, frecv,
):
    dp, pa = lax.axis_index("dp"), lax.axis_index("param")
    zh, x, y = dp // 16, (dp // 4) % 4, dp % 4
    zl, c = pa // 2, pa % 2
    z = zh * 4 + zl
    h = zl % 2
    near = zl + 1 - 2 * h
    slot = x * 4 + y

    def at_z(k):
        t = (z + k + 8) % 8
        return ((t // 4) * 16 + slot, (t % 4) * 2 + c)

    def at_xy(dx, dy):
        return (zh * 16 + ((x + dx + 4) % 4) * 4 + (y + dy + 4) % 4, pa)

    partner = (dp, zl * 2 + 1 - c)

    def remote(src, dst, ssem, rsem, dev):
        return pltpu.make_async_remote_copy(src, dst, ssem, rsem, device_id=dev, device_id_type=MESH)

    def lanes(half):
        return pl.ds(pl.multiple_of(half * HALF, 128), HALF)

    loads = [
        pltpu.make_async_copy(g_in, g, lsem.at[0]),
        pltpu.make_async_copy(iinv_in.at[:, lanes(1 - h)], iv.at[1], lsem.at[1]),
        pltpu.make_async_copy(iinv_in.at[:, lanes(h)], iv.at[0], lsem.at[2]),
        pltpu.make_async_copy(e_in, ebuf, lsem.at[3]),
        pltpu.make_async_copy(a_in.at[:, :, :, lanes(h)], abuf.at[:, zl, c], lsem.at[4]),
    ] + [
        pltpu.make_async_copy(
            oinv_in.at[pl.ds(pl.multiple_of((zl - h + k) * 320 + c * 160, 32), 160)], ob.at[pl.ds(k * 160, 160)], lsem.at[5 + k]
        )
        for k in (0, 1)
    ]
    for cp in loads:
        cp.start()

    barrier = pltpu.get_barrier_semaphore()
    for dev in (at_z(1), at_z(-1), at_z(2), at_z(-2), at_xy(1, 0), at_xy(-1, 0), at_xy(0, 1), at_xy(0, -1)):
        pl.semaphore_signal(barrier, inc=1, device_id=dev, device_id_type=MESH)
    for j in range(1, 8):
        pl.semaphore_signal(barrier, inc=1, device_id=(dp, (pa + j) % 8), device_id_type=MESH)
    pl.semaphore_wait(barrier, 15)

    both = (1, -1)

    def e_copy(k):
        ref = et.at[h, pl.ds(k * 4, 4)]
        return remote(ref, ref, esend, erecv.at[k], (dp, near * 2 + c))

    def a_near(k):
        for d in both:

            @pl.when((zl + d >= 0) & (zl + d <= 3))
            def _():
                a_copy(k, zl, a_in.at[k, :, :, lanes(1 - h)], d).start()

    def a_send(k, near=True):
        @pl.when(k < GROUPS)
        def _():
            e_copy(k).start()
            if near:
                a_near(k)
            for d in both:

                @pl.when((zl + 2 * d >= 0) & (zl + 2 * d <= 3))
                def _():
                    a_copy(k, zl, abuf.at[k, zl, c], 2 * d).start()

    def a_copy(k, block, src, d):
        return remote(src, abuf.at[k, block, c], asend, arecv.at[block, k], at_z(d))

    def a_share(k, block):
        ref = abuf.at[k, block, c]
        return remote(ref, ref, adsend, adrecv.at[block, k], partner)

    def middle(block):
        return ((zl == 1) & (block == 0)) | ((zl == 2) & (block == 3))

    def a_pass(k):
        for block in (0, 3):

            @pl.when(middle(block))
            def _():
                ref = abuf.at[k, block, c]
                a_copy(k, block, ref, 1).wait_recv()
                a_copy(k, block, ref, 2 if block == 0 else -2).start()
                a_share(k, block).start()

    def a_collect(k):
        for j in range(1, 4):
            block = (zl + j) % 4

            @pl.when(jnp.logical_not(middle(block)))
            def _():
                a_copy(k, block, abuf.at[k, block, c], 1).wait_recv()
                a_share(k, block).start()

    def a_ready(k):
        for j in range(4):
            a_share(k, (zl + j) % 4).wait_recv()
        e_copy(k).wait_recv()

    mstage, mbuf = (mstage0, mstage1, mstage2), (mbuf0, mbuf1, mbuf2)

    def m_copy(n, d, kind):
        k = (0 if d > 0 else 4) + kind
        if kind == 0:
            return remote(mstage[n], mbuf[n].at[z, c], msend.at[n, k], mrecv.at[n, k], at_z(d))
        ref = mbuf[n].at[(z - d * (kind - 1) + 8) % 8, c]
        if kind == 3:
            ref = ref.at[pl.ds(0 if d > 0 else 80, 80)]
        return remote(ref, ref, msend.at[n, k], mrecv.at[n, k], at_z(2 * d))

    def m_share(n, j, k):
        ref = mbuf[n].at[(z + j + 8) % 8, c]
        return remote(ref, ref, mdsend.at[n, k], mdrecv.at[n, k], partner)

    sent = []

    def send(cp):
        cp.start()
        sent.append(cp)

    def m_other(n):
        lo, hi = CUTS[n]
        mstage[n][...] = dot(g[...], iv[1, :, lo:hi], ((1,), (0,))).astype(BF16)

    def m_own(n):
        lo, hi = CUTS[n]
        mbuf[n][z, c] = dot(g[...], iv[0, :, lo:hi], ((1,), (0,))).astype(BF16)

    def m_first(n):
        for i, d in enumerate(both):
            m_copy(n, d, 0).wait_recv()
            send(m_copy(n, d, 2))
            send(m_share(n, -d, 1 + i))

    def m_second(n):
        for i, d in enumerate(both):
            m_copy(n, d, 1).wait_recv()
            send(m_copy(n, d, 3))
            send(m_share(n, -2 * d, 3 + i))

    def m_last(n):
        for i, d in enumerate(both):
            m_copy(n, d, 2).wait_recv()
            send(m_share(n, -3 * d, 5 + i))
        for d in both:
            m_copy(n, d, 3).wait_recv()
        send(m_share(n, 4, 7))
        for k, j in enumerate((0, -1, 1, -2, 2, -3, 3, 4)):
            m_share(n, j, k).wait_recv()

    def turn(i, carry):
        et[h, i] = ebuf[pl.ds(2 * i, 2)].reshape(128, 160).T
        return carry

    def m_start(n):
        for kind in (0, 1):
            for d in both:
                send(m_copy(n, d, kind))
        send(m_share(n, 0, 0))

    a_near(0)
    loads[0].wait()
    loads[1].wait()
    m_other(0)
    loads[2].wait()
    m_own(0)
    m_start(0)
    a_near(1)
    for n in (1, 2):
        m_other(n)
        m_own(n)
    m_first(0)
    m_second(0)
    m_start(1)
    loads[5].wait()
    loads[6].wait()

    def place(first, d1, d2):
        dx, dy = (d1, d2) if first == 0 else (d2, d1)
        return ((x + dx + 4) % 4) * 4 + (y + dy + 4) % 4

    def neighbour(first, axis, d):
        return at_xy(d, 0) if (first == axis) else at_xy(0, d)

    def x_copy(v, first, axis, d, d1, whole):
        u = 2 * v + first
        k = 0 if d > 0 else 1
        if axis == 0:
            s = place(first, 0 if whole else -d, 0)
            sem = k if whole else 2 + k
        else:
            s = place(first, d1, 0 if whole else -d)
            sem = 4 + (d1 + 1) * 4 + (k if whole else 2 + k)
        ref = w.at[u, s]
        if not whole:
            ref = ref.at[:, pl.ds(k * 2 * HALF, 2 * HALF)]
        return remote(ref, ref, xsend.at[u], xrecv.at[u, sem], neighbour(first, axis, d))

    def stage0(v):
        for d in both:
            for first in (0, 1):
                x_copy(v, first, 0, d, 0, True).start()
        for d in both:
            for first in (0, 1):
                x_copy(v, first, 1, d, 0, True).start()

    def stage1(v):
        for d in both:
            for first in (0, 1):
                x_copy(v, first, 0, d, 0, True).wait_recv()
                x_copy(v, first, 0, d, 0, False).start()
                for e in both:
                    x_copy(v, first, 1, e, -d, True).start()
        for d in both:
            for first in (0, 1):
                x_copy(v, first, 1, d, 0, True).wait_recv()
                x_copy(v, first, 1, d, 0, False).start()

    def stage2(v):
        for first in (0, 1):
            for d in both:
                x_copy(v, first, 0, d, 0, False).wait_recv()
            for e in both:
                x_copy(v, first, 1, e, 2, True).start()
        for d1 in both:
            for d in both:
                for first in (0, 1):
                    x_copy(v, first, 1, d, d1, True).wait_recv()
                    x_copy(v, first, 1, d, d1, False).start()

    def stage3(v):
        for d in both:
            for first in (0, 1):
                x_copy(v, first, 1, d, 2, True).wait_recv()
                x_copy(v, first, 1, d, 2, False).start()

    def stage4(v):
        for d1 in (0, 1, -1, 2):
            for d in both:
                for first in (0, 1):
                    x_copy(v, first, 1, d, d1, False).wait_recv()

    def precondition(n):
        lo, hi = CUTS[n]
        p = [
            dot(ob[...], mbuf[n][4 * k : 4 * k + 4].reshape(1280, hi - lo), ((1,), (0,))).reshape(40, 8, hi - lo)
            for k in (0, 1)
        ]
        p = jnp.concatenate(p, axis=1).astype(BF16)
        for i in range(lo // 128, hi // 128):
            for k in range(40):
                u, place_in = 2 * i + k // 20, 128 * (k % 20)
                w[u, slot, :, place_in : place_in + 128] = p[k, :, 128 * i - lo : 128 * i - lo + 128]

    m_last(0)
    precondition(0)
    stage0(0)
    m_first(1)
    m_second(1)
    m_start(2)
    loads[3].wait()
    loads[4].wait()
    lax.fori_loop(0, 16, turn, 0)
    m_last(1)
    precondition(1)
    stage0(1)
    stage0(2)
    m_first(2)
    m_second(2)
    stage1(0)
    for k in range(GROUPS):
        a_share(k, zl).start()
    lax.fori_loop(16, 32, turn, 0)
    a_send(jnp.int32(0), False)
    m_last(2)
    a_send(jnp.int32(1), False)
    precondition(2)
    acc[...] = jnp.zeros_like(acc)

    left_half = lax.broadcasted_iota(jnp.int32, (160, 128), 1) < 64

    def example_grads(k):
        a8 = abuf[k].astype(F32).reshape(8, 2, 4, 8, HALF)
        for pair in range(4):
            quad, i = pair // 2, 2 * (pair % 2)
            acts = jnp.concatenate([a8[:, quad, i].reshape(64, HALF), a8[:, quad, i + 1].reshape(64, HALF)], axis=0).astype(BF16)
            for cc in range(2):
                errs = et[cc, k * 4 + pair].astype(F32)
                pieces = [
                    dot(jnp.where(left_half, errs, 0.0).astype(BF16), acts, ((1,), (0,))).reshape(20, 8, HALF),
                    dot(jnp.where(left_half, 0.0, errs).astype(BF16), acts, ((1,), (0,))).reshape(20, 8, HALF),
                ]
                both_images = jnp.concatenate(pieces, axis=1).astype(BF16)
                for i in range(5):
                    for j in range(20):
                        eg[2 * i + cc, k * 4 + pair, :, j * 128 : j * 128 + 128] = both_images[j, :, i * 128 : i * 128 + 128]

    def score(v, lo, hi):
        total = acc[lo:hi]
        for u in (2 * v, 2 * v + 1):
            total += dot(eg[u, lo // 16 : hi // 16].reshape(hi - lo, WIDE), w[u].reshape(256, WIDE), ((1,), (1,)))
        acc[lo:hi] = total

    def pick(t, times):
        on, index = t == times[0], 0
        for k in range(1, len(times)):
            on = on | (t == times[k])
            index = index + jnp.where(t >= times[k], 1, 0)
        return on, index

    def score_rest(v, carry):
        score(v, LATE, 512)
        return carry

    def step(t, carry):
        on, i = pick(t, (2, 4, 7, 9, 12, 14, 17, 19))

        @pl.when(on)
        def _(i=i + 0):
            a_pass(i)

        on, i = pick(t, (2, 4, 7, 9, 12, 14))

        @pl.when(on)
        def _(i=i + 2):
            a_send(i)

        on, i = pick(t, (3, 6, 9, 12))

        @pl.when(on)
        def _(i=i + 1):
            stage1(i)

        on, i = pick(t, (0, 3))

        @pl.when(on)
        def _(i=i + 3):
            stage0(i)

        on, i = pick(t, (4, 7, 10, 13, 16))

        @pl.when(on)
        def _(i=i + 0):
            stage2(i)

        on, i = pick(t, (8, 11, 14, 17, 18))

        @pl.when(on)
        def _(i=i + 0):
            stage3(i)

        on, i = pick(t, (11, 14, 17, 18, 19))

        @pl.when(on)
        def _(i=i + 0):
            stage4(i)

        on, i = pick(t, (8, 10, 13, 15, 18, 20, 23, 25))

        @pl.when(on)
        def _(i=i + 0):
            a_collect(i)

        on, i = pick(t, (9, 11, 14, 16, 19, 21, 24, 26))

        @pl.when(on)
        def _(i=i + 0):
            a_ready(i)
            example_grads(i)

        on, i = pick(t, (16, 17, 18, 19, 20))

        @pl.when(on)
        def _(i=i + 0):
            score(i, 0, LATE)

        return carry

    lax.fori_loop(0, STEPS, step, 0)
    lax.fori_loop(0, 5, score_rest, 0)

    row = lax.broadcasted_iota(jnp.int32, (512, 256), 0)
    col = lax.broadcasted_iota(jnp.int32, (512, 256), 1)
    sums = jnp.where(row % 8 == col % 8, acc[...], 0.0).reshape(64, 8, 256).sum(axis=1)
    col = lax.broadcasted_iota(jnp.int32, (256, 128), 0)
    query = lax.broadcasted_iota(jnp.int32, (256, 128), 1)
    pick = jnp.where(((col // 8) % 2) * 16 + col // 16 == query, 1.0, 0.0).astype(F32)
    part[...] = jnp.dot(sums, pick, preferred_element_type=F32, precision=lax.Precision.HIGHEST)

    shares = []
    for j in range(1, 8):
        to = (pa + j) % 8
        cp = remote(part.at[pl.ds(pl.multiple_of(to * 8, 8), 8)], rbuf.at[j - 1], fsend.at[j - 1], frecv.at[j - 1], (dp, to))
        cp.start()
        shares.append(cp)
    total = part[pl.ds(pl.multiple_of(pa * 8, 8), 8)]
    for j in range(7):
        shares[j].wait_recv()
        total = total + rbuf[j]
    out[...] = total[:, :32] * (1.0 / (1280 * math.sqrt(64)))

    for cp in shares + sent:
        cp.wait_send()

    def all_sent(u, carry):
        ref = w.at[u, pl.ds(0, 15)]
        remote(ref, ref, xsend.at[u], xrecv.at[u, 0], partner).wait_send()
        return carry

    lax.fori_loop(0, UNITS, all_sent, 0)
    remote(et.at[0], et.at[0], esend, erecv.at[0], partner).wait_send()
    ref = abuf.at[:, :, 0]
    remote(ref, ref, adsend, arecv.at[0, 0], partner).wait_send()
    inner = (zl == 1) | (zl == 2)

    @pl.when(inner)
    def _():
        ref = abuf.at[:, :, 0]
        remote(ref, ref, asend, arecv.at[0, 0], partner).wait_send()

    @pl.when(jnp.logical_not(inner))
    def _():
        ref = abuf.at[:, pl.ds(0, 2), 0]
        remote(ref, ref, asend, arecv.at[0, 0], partner).wait_send()


def per_device(query_grads, in_inverse, out_inverse, activations, errors):
    dma = pltpu.SemaphoreType.DMA
    return pl.pallas_call(
        kernel,
        out_shape=jax.ShapeDtypeStruct((8, 32), F32),
        in_specs=[pl.BlockSpec(memory_space=pl.ANY)] * 5,
        out_specs=pl.BlockSpec(memory_space=pltpu.VMEM),
        scratch_shapes=[
            pltpu.VMEM((160, 1280), BF16),
            pltpu.VMEM((2, 1280, HALF), BF16),
            pltpu.VMEM((320, 1280), BF16),
            pltpu.VMEM((160, 128), BF16),
            pltpu.VMEM((160, 256), BF16),
            pltpu.VMEM((160, 256), BF16),
            pltpu.VMEM((8, 2, 160, 128), BF16),
            pltpu.VMEM((8, 2, 160, 256), BF16),
            pltpu.VMEM((8, 2, 160, 256), BF16),
            pltpu.VMEM((UNITS, 16, 16, WIDE), BF16),
            pltpu.VMEM((GROUPS, 4, 2, 2, 32, HALF), BF16),
            pltpu.VMEM((64, 64, 160), BF16),
            pltpu.VMEM((2, 32, 160, 128), BF16),
            pltpu.VMEM((UNITS, 32, 16, WIDE), BF16),
            pltpu.VMEM((512, 256), F32),
            pltpu.VMEM((64, 128), F32),
            pltpu.VMEM((7, 8, 128), F32),
            dma((7,)),
            dma((3, 8)),
            dma((3, 8)),
            dma((3, 8)),
            dma((3, 8)),
            dma,
            dma((GROUPS,)),
            dma((UNITS,)),
            dma((UNITS, 20)),
            dma,
            dma((4, GROUPS)),
            dma,
            dma((4, GROUPS)),
            dma((7,)),
            dma((7,)),
        ],
        compiler_params=pltpu.CompilerParams(
            collective_id=0, has_side_effects=True, vmem_limit_bytes=63 * 1024 * 1024
        ),
        cost_estimate=pl.CostEstimate(flops=4 * 10**9, bytes_accessed=10**7, transcendentals=0),
    )(
        query_grads.reshape(160, 1280),
        in_inverse,
        out_inverse,
        activations.reshape(GROUPS, 2, 32, 1280),
        errors,
    )


def solution(mesh):
    return jax.shard_map(
        per_device,
        mesh=mesh,
        in_specs=(P("dp", "param", None), P(), P(), P("dp", "param", None), P("dp", None, "param")),
        out_specs=P(("dp", "param"), None),
        check_vma=False,
    )
```

```python
import math

import jax
import jax.numpy as jnp
from jax import lax
from jax.experimental import pallas as pl
from jax.experimental.pallas import tpu as pltpu
from jax.sharding import PartitionSpec as P

MESH = pl.DeviceIdType.MESH
BF16 = jnp.bfloat16
F32 = jnp.float32
GROUPS = 8
STEPS = 26
LATE = 256
UNITS = 10
HALF = 640
WIDE = 20 * 128
CUTS = ((0, 128), (128, 384), (384, 640))


def dot(a, b, dims):
    return lax.dot_general(a, b, (dims, ((), ())), preferred_element_type=F32)


def kernel(
    g_in, iinv_in, oinv_in, a_in, e_in, out,
    g, iv, ob, mstage0, mstage1, mstage2, mbuf0, mbuf1, mbuf2, w, abuf, ebuf, et, eg, acc, part, rbuf,
    lsem, msend, mrecv, mdsend, mdrecv, esend, erecv, xsend, xrecv, asend, arecv, adsend, adrecv, fsend, frecv,
):
    dp, pa = lax.axis_index("dp"), lax.axis_index("param")
    zh, x, y = dp // 16, (dp // 4) % 4, dp % 4
    zl, c = pa // 2, pa % 2
    z = zh * 4 + zl
    h = zl % 2
    near = zl + 1 - 2 * h
    slot = x * 4 + y

    def at_z(k):
        t = (z + k + 8) % 8
        return ((t // 4) * 16 + slot, (t % 4) * 2 + c)

    def at_xy(dx, dy):
        return (zh * 16 + ((x + dx + 4) % 4) * 4 + (y + dy + 4) % 4, pa)

    partner = (dp, zl * 2 + 1 - c)

    def remote(src, dst, ssem, rsem, dev):
        return pltpu.make_async_remote_copy(src, dst, ssem, rsem, device_id=dev, device_id_type=MESH)

    def lanes(half):
        return pl.ds(pl.multiple_of(half * HALF, 128), HALF)

    loads = [
        pltpu.make_async_copy(g_in, g, lsem.at[0]),
        pltpu.make_async_copy(iinv_in.at[:, lanes(1 - h)], iv.at[1], lsem.at[1]),
        pltpu.make_async_copy(iinv_in.at[:, lanes(h)], iv.at[0], lsem.at[2]),
        pltpu.make_async_copy(e_in, ebuf, lsem.at[3]),
        pltpu.make_async_copy(a_in.at[:, :, :, lanes(h)], abuf.at[:, zl, c], lsem.at[4]),
    ] + [
        pltpu.make_async_copy(
            oinv_in.at[pl.ds(pl.multiple_of((zl - h + k) * 320 + c * 160, 32), 160)], ob.at[pl.ds(k * 160, 160)], lsem.at[5 + k]
        )
        for k in (0, 1)
    ]
    for cp in loads:
        cp.start()

    barrier = pltpu.get_barrier_semaphore()
    for dev in (at_z(1), at_z(-1), at_z(2), at_z(-2), at_xy(1, 0), at_xy(-1, 0), at_xy(0, 1), at_xy(0, -1)):
        pl.semaphore_signal(barrier, inc=1, device_id=dev, device_id_type=MESH)
    for j in range(1, 8):
        pl.semaphore_signal(barrier, inc=1, device_id=(dp, (pa + j) % 8), device_id_type=MESH)
    pl.semaphore_wait(barrier, 15)

    both = (1, -1)

    def e_copy(k):
        ref = et.at[h, pl.ds(k * 4, 4)]
        return remote(ref, ref, esend, erecv.at[k], (dp, near * 2 + c))

    def a_near(k):
        for d in both:

            @pl.when((zl + d >= 0) & (zl + d <= 3))
            def _():
                a_copy(k, zl, a_in.at[k, :, :, lanes(1 - h)], d).start()

    def a_send(k, near=True):
        @pl.when(k < GROUPS)
        def _():
            e_copy(k).start()
            if near:
                a_near(k)
            for d in both:

                @pl.when((zl + 2 * d >= 0) & (zl + 2 * d <= 3))
                def _():
                    a_copy(k, zl, abuf.at[k, zl, c], 2 * d).start()

    def a_copy(k, block, src, d):
        return remote(src, abuf.at[k, block, c], asend, arecv.at[block, k], at_z(d))

    def a_share(k, block):
        ref = abuf.at[k, block, c]
        return remote(ref, ref, adsend, adrecv.at[block, k], partner)

    def middle(block):
        return ((zl == 1) & (block == 0)) | ((zl == 2) & (block == 3))

    def a_pass(k):
        for block in (0, 3):

            @pl.when(middle(block))
            def _():
                ref = abuf.at[k, block, c]
                a_copy(k, block, ref, 1).wait_recv()
                a_copy(k, block, ref, 2 if block == 0 else -2).start()
                a_share(k, block).start()

    def a_collect(k):
        for j in range(1, 4):
            block = (zl + j) % 4

            @pl.when(jnp.logical_not(middle(block)))
            def _():
                a_copy(k, block, abuf.at[k, block, c], 1).wait_recv()
                a_share(k, block).start()

    def a_ready(k):
        for j in range(4):
            a_share(k, (zl + j) % 4).wait_recv()
        e_copy(k).wait_recv()

    mstage, mbuf = (mstage0, mstage1, mstage2), (mbuf0, mbuf1, mbuf2)

    def m_copy(n, d, kind):
        k = (0 if d > 0 else 4) + kind
        if kind == 0:
            return remote(mstage[n], mbuf[n].at[z, c], msend.at[n, k], mrecv.at[n, k], at_z(d))
        ref = mbuf[n].at[(z - d * (kind - 1) + 8) % 8, c]
        if kind == 3:
            ref = ref.at[pl.ds(0 if d > 0 else 80, 80)]
        return remote(ref, ref, msend.at[n, k], mrecv.at[n, k], at_z(2 * d))

    def m_share(n, j, k):
        ref = mbuf[n].at[(z + j + 8) % 8, c]
        return remote(ref, ref, mdsend.at[n, k], mdrecv.at[n, k], partner)

    sent = []

    def send(cp):
        cp.start()
        sent.append(cp)

    def m_other(n):
        lo, hi = CUTS[n]
        mstage[n][...] = dot(g[...], iv[1, :, lo:hi], ((1,), (0,))).astype(BF16)

    def m_own(n):
        lo, hi = CUTS[n]
        mbuf[n][z, c] = dot(g[...], iv[0, :, lo:hi], ((1,), (0,))).astype(BF16)

    def m_first(n):
        for i, d in enumerate(both):
            m_copy(n, d, 0).wait_recv()
            send(m_copy(n, d, 2))
            send(m_share(n, -d, 1 + i))

    def m_second(n):
        for i, d in enumerate(both):
            m_copy(n, d, 1).wait_recv()
            send(m_copy(n, d, 3))
            send(m_share(n, -2 * d, 3 + i))

    def m_last(n):
        for i, d in enumerate(both):
            m_copy(n, d, 2).wait_recv()
            send(m_share(n, -3 * d, 5 + i))
        for d in both:
            m_copy(n, d, 3).wait_recv()
        send(m_share(n, 4, 7))
        for k, j in enumerate((0, -1, 1, -2, 2, -3, 3, 4)):
            m_share(n, j, k).wait_recv()

    def turn(i, carry):
        et[h, i] = ebuf[pl.ds(2 * i, 2)].reshape(128, 160).T
        return carry

    def m_start(n):
        for kind in (0, 1):
            for d in both:
                send(m_copy(n, d, kind))
        send(m_share(n, 0, 0))

    a_near(0)
    loads[0].wait()
    loads[1].wait()
    m_other(0)
    loads[2].wait()
    m_own(0)
    m_start(0)
    a_near(1)
    for n in (1, 2):
        m_other(n)
        m_own(n)
    m_first(0)
    m_second(0)
    m_start(1)
    loads[5].wait()
    loads[6].wait()

    def place(first, d1, d2):
        dx, dy = (d1, d2) if first == 0 else (d2, d1)
        return ((x + dx + 4) % 4) * 4 + (y + dy + 4) % 4

    def neighbour(first, axis, d):
        return at_xy(d, 0) if (first == axis) else at_xy(0, d)

    def x_copy(v, first, axis, d, d1, whole):
        u = 2 * v + first
        k = 0 if d > 0 else 1
        if axis == 0:
            s = place(first, 0 if whole else -d, 0)
            sem = k if whole else 2 + k
        else:
            s = place(first, d1, 0 if whole else -d)
            sem = 4 + (d1 + 1) * 4 + (k if whole else 2 + k)
        ref = w.at[u, s]
        if not whole:
            ref = ref.at[:, pl.ds(k * 2 * HALF, 2 * HALF)]
        return remote(ref, ref, xsend.at[u], xrecv.at[u, sem], neighbour(first, axis, d))

    def stage0(v):
        for d in both:
            for first in (0, 1):
                x_copy(v, first, 0, d, 0, True).start()
        for d in both:
            for first in (0, 1):
                x_copy(v, first, 1, d, 0, True).start()

    def stage1(v):
        for d in both:
            for first in (0, 1):
                x_copy(v, first, 0, d, 0, True).wait_recv()
                x_copy(v, first, 0, d, 0, False).start()
                for e in both:
                    x_copy(v, first, 1, e, -d, True).start()
        for d in both:
            for first in (0, 1):
                x_copy(v, first, 1, d, 0, True).wait_recv()
                x_copy(v, first, 1, d, 0, False).start()

    def stage2(v):
        for first in (0, 1):
            for d in both:
                x_copy(v, first, 0, d, 0, False).wait_recv()
            for e in both:
                x_copy(v, first, 1, e, 2, True).start()
        for d1 in both:
            for d in both:
                for first in (0, 1):
                    x_copy(v, first, 1, d, d1, True).wait_recv()
                    x_copy(v, first, 1, d, d1, False).start()

    def stage3(v):
        for d in both:
            for first in (0, 1):
                x_copy(v, first, 1, d, 2, True).wait_recv()
                x_copy(v, first, 1, d, 2, False).start()

    def stage4(v):
        for d1 in (0, 1, -1, 2):
            for d in both:
                for first in (0, 1):
                    x_copy(v, first, 1, d, d1, False).wait_recv()

    def precondition(n):
        lo, hi = CUTS[n]
        p = [
            dot(ob[...], mbuf[n][4 * k : 4 * k + 4].reshape(1280, hi - lo), ((1,), (0,))).reshape(40, 8, hi - lo)
            for k in (0, 1)
        ]
        p = jnp.concatenate(p, axis=1).astype(BF16)
        for i in range(lo // 128, hi // 128):
            for k in range(40):
                u, place_in = 2 * i + k // 20, 128 * (k % 20)
                w[u, slot, :, place_in : place_in + 128] = p[k, :, 128 * i - lo : 128 * i - lo + 128]

    m_last(0)
    precondition(0)
    stage0(0)
    m_first(1)
    m_second(1)
    m_start(2)
    loads[3].wait()
    loads[4].wait()
    lax.fori_loop(0, 16, turn, 0)
    m_last(1)
    precondition(1)
    stage0(1)
    stage0(2)
    m_first(2)
    m_second(2)
    stage1(0)
    for k in range(GROUPS):
        a_share(k, zl).start()
    lax.fori_loop(16, 32, turn, 0)
    a_send(jnp.int32(0), False)
    m_last(2)
    a_send(jnp.int32(1), False)
    precondition(2)
    acc[...] = jnp.zeros_like(acc)

    left_half = lax.broadcasted_iota(jnp.int32, (160, 128), 1) < 64

    def example_grads(k):
        a8 = abuf[k].astype(F32).reshape(8, 2, 4, 8, HALF)
        for pair in range(4):
            quad, i = pair // 2, 2 * (pair % 2)
            acts = jnp.concatenate([a8[:, quad, i].reshape(64, HALF), a8[:, quad, i + 1].reshape(64, HALF)], axis=0).astype(BF16)
            for cc in range(2):
                errs = et[cc, k * 4 + pair].astype(F32)
                pieces = [
                    dot(jnp.where(left_half, errs, 0.0).astype(BF16), acts, ((1,), (0,))).reshape(20, 8, HALF),
                    dot(jnp.where(left_half, 0.0, errs).astype(BF16), acts, ((1,), (0,))).reshape(20, 8, HALF),
                ]
                both_images = jnp.concatenate(pieces, axis=1).astype(BF16)
                for i in range(5):
                    for j in range(20):
                        eg[2 * i + cc, k * 4 + pair, :, j * 128 : j * 128 + 128] = both_images[j, :, i * 128 : i * 128 + 128]

    def score(v, lo, hi):
        total = acc[lo:hi]
        for u in (2 * v, 2 * v + 1):
            total += dot(eg[u, lo // 16 : hi // 16].reshape(hi - lo, WIDE), w[u].reshape(256, WIDE), ((1,), (1,)))
        acc[lo:hi] = total

    def pick(t, times):
        on, index = t == times[0], 0
        for k in range(1, len(times)):
            on = on | (t == times[k])
            index = index + jnp.where(t >= times[k], 1, 0)
        return on, index

    def score_rest(v, carry):
        score(v, LATE, 512)
        return carry

    def step(t, carry):
        on, i = pick(t, (2, 4, 7, 9, 12, 14, 17, 19))

        @pl.when(on)
        def _(i=i + 0):
            a_pass(i)

        on, i = pick(t, (2, 4, 7, 9, 12, 14))

        @pl.when(on)
        def _(i=i + 2):
            a_send(i)

        on, i = pick(t, (3, 6, 9, 12))

        @pl.when(on)
        def _(i=i + 1):
            stage1(i)

        on, i = pick(t, (0, 3))

        @pl.when(on)
        def _(i=i + 3):
            stage0(i)

        on, i = pick(t, (4, 7, 10, 13, 16))

        @pl.when(on)
        def _(i=i + 0):
            stage2(i)

        on, i = pick(t, (8, 11, 14, 17, 18))

        @pl.when(on)
        def _(i=i + 0):
            stage3(i)

        on, i = pick(t, (11, 14, 17, 18, 19))

        @pl.when(on)
        def _(i=i + 0):
            stage4(i)

        on, i = pick(t, (7, 9, 12, 14, 17, 19, 22, 24))

        @pl.when(on)
        def _(i=i + 0):
            a_collect(i)

        on, i = pick(t, (8, 10, 13, 15, 18, 20, 23, 25))

        @pl.when(on)
        def _(i=i + 0):
            a_ready(i)
            example_grads(i)

        on, i = pick(t, (15, 16, 17, 18, 19))

        @pl.when(on)
        def _(i=i + 0):
            score(i, 0, LATE)

        return carry

    lax.fori_loop(0, STEPS, step, 0)
    lax.fori_loop(0, 5, score_rest, 0)

    row = lax.broadcasted_iota(jnp.int32, (512, 256), 0)
    col = lax.broadcasted_iota(jnp.int32, (512, 256), 1)
    sums = jnp.where(row % 8 == col % 8, acc[...], 0.0).reshape(64, 8, 256).sum(axis=1)
    col = lax.broadcasted_iota(jnp.int32, (256, 128), 0)
    query = lax.broadcasted_iota(jnp.int32, (256, 128), 1)
    pick = jnp.where(((col // 8) % 2) * 16 + col // 16 == query, 1.0, 0.0).astype(F32)
    part[...] = jnp.dot(sums, pick, preferred_element_type=F32, precision=lax.Precision.HIGHEST)

    shares = []
    for j in range(1, 8):
        to = (pa + j) % 8
        cp = remote(part.at[pl.ds(pl.multiple_of(to * 8, 8), 8)], rbuf.at[j - 1], fsend.at[j - 1], frecv.at[j - 1], (dp, to))
        cp.start()
        shares.append(cp)
    total = part[pl.ds(pl.multiple_of(pa * 8, 8), 8)]
    for j in range(7):
        shares[j].wait_recv()
        total = total + rbuf[j]
    out[...] = total[:, :32] * (1.0 / (1280 * math.sqrt(64)))

    for cp in shares + sent:
        cp.wait_send()

    def all_sent(u, carry):
        ref = w.at[u, pl.ds(0, 15)]
        remote(ref, ref, xsend.at[u], xrecv.at[u, 0], partner).wait_send()
        return carry

    lax.fori_loop(0, UNITS, all_sent, 0)
    remote(et.at[0], et.at[0], esend, erecv.at[0], partner).wait_send()
    ref = abuf.at[:, :, 0]
    remote(ref, ref, adsend, arecv.at[0, 0], partner).wait_send()
    inner = (zl == 1) | (zl == 2)

    @pl.when(inner)
    def _():
        ref = abuf.at[:, :, 0]
        remote(ref, ref, asend, arecv.at[0, 0], partner).wait_send()

    @pl.when(jnp.logical_not(inner))
    def _():
        ref = abuf.at[:, pl.ds(0, 2), 0]
        remote(ref, ref, asend, arecv.at[0, 0], partner).wait_send()


def per_device(query_grads, in_inverse, out_inverse, activations, errors):
    dma = pltpu.SemaphoreType.DMA
    return pl.pallas_call(
        kernel,
        out_shape=jax.ShapeDtypeStruct((8, 32), F32),
        in_specs=[pl.BlockSpec(memory_space=pl.ANY)] * 5,
        out_specs=pl.BlockSpec(memory_space=pltpu.VMEM),
        scratch_shapes=[
            pltpu.VMEM((160, 1280), BF16),
            pltpu.VMEM((2, 1280, HALF), BF16),
            pltpu.VMEM((320, 1280), BF16),
            pltpu.VMEM((160, 128), BF16),
            pltpu.VMEM((160, 256), BF16),
            pltpu.VMEM((160, 256), BF16),
            pltpu.VMEM((8, 2, 160, 128), BF16),
            pltpu.VMEM((8, 2, 160, 256), BF16),
            pltpu.VMEM((8, 2, 160, 256), BF16),
            pltpu.VMEM((UNITS, 16, 16, WIDE), BF16),
            pltpu.VMEM((GROUPS, 4, 2, 2, 32, HALF), BF16),
            pltpu.VMEM((64, 64, 160), BF16),
            pltpu.VMEM((2, 32, 160, 128), BF16),
            pltpu.VMEM((UNITS, 32, 16, WIDE), BF16),
            pltpu.VMEM((512, 256), F32),
            pltpu.VMEM((64, 128), F32),
            pltpu.VMEM((7, 8, 128), F32),
            dma((7,)),
            dma((3, 8)),
            dma((3, 8)),
            dma((3, 8)),
            dma((3, 8)),
            dma,
            dma((GROUPS,)),
            dma((UNITS,)),
            dma((UNITS, 20)),
            dma,
            dma((4, GROUPS)),
            dma,
            dma((4, GROUPS)),
            dma((7,)),
            dma((7,)),
        ],
        compiler_params=pltpu.CompilerParams(
            collective_id=0, has_side_effects=True, vmem_limit_bytes=63 * 1024 * 1024
        ),
        cost_estimate=pl.CostEstimate(flops=4 * 10**9, bytes_accessed=10**7, transcendentals=0),
    )(
        query_grads.reshape(160, 1280),
        in_inverse,
        out_inverse,
        activations.reshape(GROUPS, 2, 32, 1280),
        errors,
    )


def solution(mesh):
    return jax.shard_map(
        per_device,
        mesh=mesh,
        in_specs=(P("dp", "param", None), P(), P(), P("dp", "param", None), P("dp", None, "param")),
        out_specs=P(("dp", "param"), None),
        check_vma=False,
    )
```

```python
import math

import jax
import jax.numpy as jnp
from jax import lax
from jax.experimental import pallas as pl
from jax.experimental.pallas import tpu as pltpu
from jax.sharding import PartitionSpec as P

MESH = pl.DeviceIdType.MESH
BF16 = jnp.bfloat16
F32 = jnp.float32
GROUPS = 8
STEPS = 30
LATE = 256
UNITS = 10
HALF = 640
WIDE = 20 * 128
CUTS = ((0, 128), (128, 384), (384, 640))


def dot(a, b, dims):
    return lax.dot_general(a, b, (dims, ((), ())), preferred_element_type=F32)


def kernel(
    g_in, iinv_in, oinv_in, a_in, e_in, out,
    g, iv, ob, mstage0, mstage1, mstage2, mbuf0, mbuf1, mbuf2, w, abuf, ebuf, et, eg, acc, part, rbuf,
    lsem, msend, mrecv, mdsend, mdrecv, esend, erecv, xsend, xrecv, asend, arecv, adsend, adrecv, fsend, frecv,
):
    dp, pa = lax.axis_index("dp"), lax.axis_index("param")
    zh, x, y = dp // 16, (dp // 4) % 4, dp % 4
    zl, c = pa // 2, pa % 2
    z = zh * 4 + zl
    h = zl % 2
    near = zl + 1 - 2 * h
    slot = x * 4 + y

    def at_z(k):
        t = (z + k + 8) % 8
        return ((t // 4) * 16 + slot, (t % 4) * 2 + c)

    def at_xy(dx, dy):
        return (zh * 16 + ((x + dx + 4) % 4) * 4 + (y + dy + 4) % 4, pa)

    partner = (dp, zl * 2 + 1 - c)

    def remote(src, dst, ssem, rsem, dev):
        return pltpu.make_async_remote_copy(src, dst, ssem, rsem, device_id=dev, device_id_type=MESH)

    def lanes(half):
        return pl.ds(pl.multiple_of(half * HALF, 128), HALF)

    loads = [
        pltpu.make_async_copy(g_in, g, lsem.at[0]),
        pltpu.make_async_copy(iinv_in.at[:, lanes(1 - h)], iv.at[1], lsem.at[1]),
        pltpu.make_async_copy(iinv_in.at[:, lanes(h)], iv.at[0], lsem.at[2]),
        pltpu.make_async_copy(e_in, ebuf, lsem.at[3]),
        pltpu.make_async_copy(a_in.at[:, :, :, lanes(h)], abuf.at[:, zl, c], lsem.at[4]),
    ] + [
        pltpu.make_async_copy(
            oinv_in.at[pl.ds(pl.multiple_of((zl - h + k) * 320 + c * 160, 32), 160)], ob.at[pl.ds(k * 160, 160)], lsem.at[5 + k]
        )
        for k in (0, 1)
    ]
    for cp in loads:
        cp.start()

    barrier = pltpu.get_barrier_semaphore()
    for dev in (at_z(1), at_z(-1), at_z(2), at_z(-2), at_xy(1, 0), at_xy(-1, 0), at_xy(0, 1), at_xy(0, -1)):
        pl.semaphore_signal(barrier, inc=1, device_id=dev, device_id_type=MESH)
    for j in range(1, 8):
        pl.semaphore_signal(barrier, inc=1, device_id=(dp, (pa + j) % 8), device_id_type=MESH)
    pl.semaphore_wait(barrier, 15)

    both = (1, -1)

    def e_copy(k):
        ref = et.at[h, pl.ds(k * 4, 4)]
        return remote(ref, ref, esend, erecv.at[k], (dp, near * 2 + c))

    def a_near(k):
        for d in both:

            @pl.when((zl + d >= 0) & (zl + d <= 3))
            def _():
                a_copy(k, zl, a_in.at[k, :, :, lanes(1 - h)], d).start()

    def a_send(k, near=True):
        @pl.when(k < GROUPS)
        def _():
            e_copy(k).start()
            if near:
                a_near(k)
            for d in both:

                @pl.when((zl + 2 * d >= 0) & (zl + 2 * d <= 3))
                def _():
                    a_copy(k, zl, abuf.at[k, zl, c], 2 * d).start()

    def a_copy(k, block, src, d):
        return remote(src, abuf.at[k, block, c], asend, arecv.at[block, k], at_z(d))

    def a_share(k, block):
        ref = abuf.at[k, block, c]
        return remote(ref, ref, adsend, adrecv.at[block, k], partner)

    def middle(block):
        return ((zl == 1) & (block == 0)) | ((zl == 2) & (block == 3))

    def a_pass(k):
        for block in (0, 3):

            @pl.when(middle(block))
            def _():
                ref = abuf.at[k, block, c]
                a_copy(k, block, ref, 1).wait_recv()
                a_copy(k, block, ref, 2 if block == 0 else -2).start()
                a_share(k, block).start()

    def a_collect(k):
        for j in range(1, 4):
            block = (zl + j) % 4

            @pl.when(jnp.logical_not(middle(block)))
            def _():
                a_copy(k, block, abuf.at[k, block, c], 1).wait_recv()
                a_share(k, block).start()

    def a_ready(k):
        for j in range(4):
            a_share(k, (zl + j) % 4).wait_recv()
        e_copy(k).wait_recv()

    mstage, mbuf = (mstage0, mstage1, mstage2), (mbuf0, mbuf1, mbuf2)

    def m_copy(n, d, kind):
        k = (0 if d > 0 else 4) + kind
        if kind == 0:
            return remote(mstage[n], mbuf[n].at[z, c], msend.at[n, k], mrecv.at[n, k], at_z(d))
        ref = mbuf[n].at[(z - d * (kind - 1) + 8) % 8, c]
        if kind == 3:
            ref = ref.at[pl.ds(0 if d > 0 else 80, 80)]
        return remote(ref, ref, msend.at[n, k], mrecv.at[n, k], at_z(2 * d))

    def m_share(n, j, k):
        ref = mbuf[n].at[(z + j + 8) % 8, c]
        return remote(ref, ref, mdsend.at[n, k], mdrecv.at[n, k], partner)

    sent = []

    def send(cp):
        cp.start()
        sent.append(cp)

    def m_other(n):
        lo, hi = CUTS[n]
        mstage[n][...] = dot(g[...], iv[1, :, lo:hi], ((1,), (0,))).astype(BF16)

    def m_own(n):
        lo, hi = CUTS[n]
        mbuf[n][z, c] = dot(g[...], iv[0, :, lo:hi], ((1,), (0,))).astype(BF16)

    def m_first(n):
        for i, d in enumerate(both):
            m_copy(n, d, 0).wait_recv()
            send(m_copy(n, d, 2))
            send(m_share(n, -d, 1 + i))

    def m_second(n):
        for i, d in enumerate(both):
            m_copy(n, d, 1).wait_recv()
            send(m_copy(n, d, 3))
            send(m_share(n, -2 * d, 3 + i))

    def m_last(n):
        for i, d in enumerate(both):
            m_copy(n, d, 2).wait_recv()
            send(m_share(n, -3 * d, 5 + i))
        for d in both:
            m_copy(n, d, 3).wait_recv()
        send(m_share(n, 4, 7))
        for k, j in enumerate((0, -1, 1, -2, 2, -3, 3, 4)):
            m_share(n, j, k).wait_recv()

    def turn(i, carry):
        et[h, i] = ebuf[pl.ds(2 * i, 2)].reshape(128, 160).T
        return carry

    def m_start(n):
        for kind in (0, 1):
            for d in both:
                send(m_copy(n, d, kind))
        send(m_share(n, 0, 0))

    a_near(0)
    loads[0].wait()
    loads[1].wait()
    m_other(0)
    loads[2].wait()
    m_own(0)
    m_start(0)
    a_near(1)
    for n in (1, 2):
        m_other(n)
        m_own(n)
    m_first(0)
    m_second(0)
    m_start(1)
    loads[5].wait()
    loads[6].wait()

    def place(first, d1, d2):
        dx, dy = (d1, d2) if first == 0 else (d2, d1)
        return ((x + dx + 4) % 4) * 4 + (y + dy + 4) % 4

    def neighbour(first, axis, d):
        return at_xy(d, 0) if (first == axis) else at_xy(0, d)

    def x_copy(v, first, axis, d, d1, whole):
        u = 2 * v + first
        k = 0 if d > 0 else 1
        if axis == 0:
            s = place(first, 0 if whole else -d, 0)
            sem = k if whole else 2 + k
        else:
            s = place(first, d1, 0 if whole else -d)
            sem = 4 + (d1 + 1) * 4 + (k if whole else 2 + k)
        ref = w.at[u, s]
        if not whole:
            ref = ref.at[:, pl.ds(k * 2 * HALF, 2 * HALF)]
        return remote(ref, ref, xsend.at[u], xrecv.at[u, sem], neighbour(first, axis, d))

    def stage0(v):
        for d in both:
            for first in (0, 1):
                x_copy(v, first, 0, d, 0, True).start()
        for d in both:
            for first in (0, 1):
                x_copy(v, first, 1, d, 0, True).start()

    def stage1(v):
        for d in both:
            for first in (0, 1):
                x_copy(v, first, 0, d, 0, True).wait_recv()
                x_copy(v, first, 0, d, 0, False).start()
                for e in both:
                    x_copy(v, first, 1, e, -d, True).start()
        for d in both:
            for first in (0, 1):
                x_copy(v, first, 1, d, 0, True).wait_recv()
                x_copy(v, first, 1, d, 0, False).start()

    def stage2(v):
        for first in (0, 1):
            for d in both:
                x_copy(v, first, 0, d, 0, False).wait_recv()
            for e in both:
                x_copy(v, first, 1, e, 2, True).start()
        for d1 in both:
            for d in both:
                for first in (0, 1):
                    x_copy(v, first, 1, d, d1, True).wait_recv()
                    x_copy(v, first, 1, d, d1, False).start()

    def stage3(v):
        for d in both:
            for first in (0, 1):
                x_copy(v, first, 1, d, 2, True).wait_recv()
                x_copy(v, first, 1, d, 2, False).start()

    def stage4(v):
        for d1 in (0, 1, -1, 2):
            for d in both:
                for first in (0, 1):
                    x_copy(v, first, 1, d, d1, False).wait_recv()

    def precondition(n):
        lo, hi = CUTS[n]
        p = [
            dot(ob[...], mbuf[n][4 * k : 4 * k + 4].reshape(1280, hi - lo), ((1,), (0,))).reshape(40, 8, hi - lo)
            for k in (0, 1)
        ]
        p = jnp.concatenate(p, axis=1).astype(BF16)
        for i in range(lo // 128, hi // 128):
            for k in range(40):
                u, place_in = 2 * i + k // 20, 128 * (k % 20)
                w[u, slot, :, place_in : place_in + 128] = p[k, :, 128 * i - lo : 128 * i - lo + 128]

    m_last(0)
    precondition(0)
    stage0(0)
    m_first(1)
    m_second(1)
    m_start(2)
    loads[3].wait()
    loads[4].wait()
    lax.fori_loop(0, 16, turn, 0)
    m_last(1)
    precondition(1)
    stage0(1)
    stage0(2)
    m_first(2)
    m_second(2)
    stage1(0)
    for k in range(GROUPS):
        a_share(k, zl).start()
    lax.fori_loop(16, 32, turn, 0)
    a_send(jnp.int32(0), False)
    m_last(2)
    a_send(jnp.int32(1), False)
    precondition(2)
    acc[...] = jnp.zeros_like(acc)

    left_half = lax.broadcasted_iota(jnp.int32, (160, 128), 1) < 64

    def example_grads(k):
        a8 = abuf[k].astype(F32).reshape(8, 2, 4, 8, HALF)
        for pair in range(4):
            quad, i = pair // 2, 2 * (pair % 2)
            acts = jnp.concatenate([a8[:, quad, i].reshape(64, HALF), a8[:, quad, i + 1].reshape(64, HALF)], axis=0).astype(BF16)
            for cc in range(2):
                errs = et[cc, k * 4 + pair].astype(F32)
                pieces = [
                    dot(jnp.where(left_half, errs, 0.0).astype(BF16), acts, ((1,), (0,))).reshape(20, 8, HALF),
                    dot(jnp.where(left_half, 0.0, errs).astype(BF16), acts, ((1,), (0,))).reshape(20, 8, HALF),
                ]
                both_images = jnp.concatenate(pieces, axis=1).astype(BF16)
                for i in range(5):
                    for j in range(20):
                        eg[2 * i + cc, k * 4 + pair, :, j * 128 : j * 128 + 128] = both_images[j, :, i * 128 : i * 128 + 128]

    def score(v, lo, hi):
        total = acc[lo:hi]
        for u in (2 * v, 2 * v + 1):
            total += dot(eg[u, lo // 16 : hi // 16].reshape(hi - lo, WIDE), w[u].reshape(256, WIDE), ((1,), (1,)))
        acc[lo:hi] = total

    def pick(t, times):
        on, index = t == times[0], 0
        for k in range(1, len(times)):
            on = on | (t == times[k])
            index = index + jnp.where(t >= times[k], 1, 0)
        return on, index

    def score_rest(v, carry):
        score(v, LATE, 512)
        return carry

    def step(t, carry):
        on, i = pick(t, (2, 5, 8, 11, 14, 17, 20, 23))

        @pl.when(on)
        def _(i=i + 0):
            a_pass(i)

        on, i = pick(t, (2, 5, 8, 11, 14, 17))

        @pl.when(on)
        def _(i=i + 2):
            a_send(i)

        on, i = pick(t, (4, 8, 12, 16))

        @pl.when(on)
        def _(i=i + 1):
            stage1(i)

        on, i = pick(t, (0, 4))

        @pl.when(on)
        def _(i=i + 3):
            stage0(i)

        on, i = pick(t, (5, 9, 13, 17, 21))

        @pl.when(on)
        def _(i=i + 0):
            stage2(i)

        on, i = pick(t, (10, 14, 18, 22, 23))

        @pl.when(on)
        def _(i=i + 0):
            stage3(i)

        on, i = pick(t, (14, 18, 22, 23, 24))

        @pl.when(on)
        def _(i=i + 0):
            stage4(i)

        on, i = pick(t, (7, 10, 13, 16, 19, 22, 25, 28))

        @pl.when(on)
        def _(i=i + 0):
            a_collect(i)

        on, i = pick(t, (8, 11, 14, 17, 20, 23, 26, 29))

        @pl.when(on)
        def _(i=i + 0):
            a_ready(i)
            example_grads(i)

        on, i = pick(t, (17, 18, 22, 23, 24))

        @pl.when(on)
        def _(i=i + 0):
            score(i, 0, LATE)

        return carry

    lax.fori_loop(0, STEPS, step, 0)
    lax.fori_loop(0, 5, score_rest, 0)

    row = lax.broadcasted_iota(jnp.int32, (512, 256), 0)
    col = lax.broadcasted_iota(jnp.int32, (512, 256), 1)
    sums = jnp.where(row % 8 == col % 8, acc[...], 0.0).reshape(64, 8, 256).sum(axis=1)
    col = lax.broadcasted_iota(jnp.int32, (256, 128), 0)
    query = lax.broadcasted_iota(jnp.int32, (256, 128), 1)
    pick = jnp.where(((col // 8) % 2) * 16 + col // 16 == query, 1.0, 0.0).astype(F32)
    part[...] = jnp.dot(sums, pick, preferred_element_type=F32, precision=lax.Precision.HIGHEST)

    shares = []
    for j in range(1, 8):
        to = (pa + j) % 8
        cp = remote(part.at[pl.ds(pl.multiple_of(to * 8, 8), 8)], rbuf.at[j - 1], fsend.at[j - 1], frecv.at[j - 1], (dp, to))
        cp.start()
        shares.append(cp)
    total = part[pl.ds(pl.multiple_of(pa * 8, 8), 8)]
    for j in range(7):
        shares[j].wait_recv()
        total = total + rbuf[j]
    out[...] = total[:, :32] * (1.0 / (1280 * math.sqrt(64)))

    for cp in shares + sent:
        cp.wait_send()

    def all_sent(u, carry):
        ref = w.at[u, pl.ds(0, 15)]
        remote(ref, ref, xsend.at[u], xrecv.at[u, 0], partner).wait_send()
        return carry

    lax.fori_loop(0, UNITS, all_sent, 0)
    remote(et.at[0], et.at[0], esend, erecv.at[0], partner).wait_send()
    ref = abuf.at[:, :, 0]
    remote(ref, ref, adsend, arecv.at[0, 0], partner).wait_send()
    inner = (zl == 1) | (zl == 2)

    @pl.when(inner)
    def _():
        ref = abuf.at[:, :, 0]
        remote(ref, ref, asend, arecv.at[0, 0], partner).wait_send()

    @pl.when(jnp.logical_not(inner))
    def _():
        ref = abuf.at[:, pl.ds(0, 2), 0]
        remote(ref, ref, asend, arecv.at[0, 0], partner).wait_send()


def per_device(query_grads, in_inverse, out_inverse, activations, errors):
    dma = pltpu.SemaphoreType.DMA
    return pl.pallas_call(
        kernel,
        out_shape=jax.ShapeDtypeStruct((8, 32), F32),
        in_specs=[pl.BlockSpec(memory_space=pl.ANY)] * 5,
        out_specs=pl.BlockSpec(memory_space=pltpu.VMEM),
        scratch_shapes=[
            pltpu.VMEM((160, 1280), BF16),
            pltpu.VMEM((2, 1280, HALF), BF16),
            pltpu.VMEM((320, 1280), BF16),
            pltpu.VMEM((160, 128), BF16),
            pltpu.VMEM((160, 256), BF16),
            pltpu.VMEM((160, 256), BF16),
            pltpu.VMEM((8, 2, 160, 128), BF16),
            pltpu.VMEM((8, 2, 160, 256), BF16),
            pltpu.VMEM((8, 2, 160, 256), BF16),
            pltpu.VMEM((UNITS, 16, 16, WIDE), BF16),
            pltpu.VMEM((GROUPS, 4, 2, 2, 32, HALF), BF16),
            pltpu.VMEM((64, 64, 160), BF16),
            pltpu.VMEM((2, 32, 160, 128), BF16),
            pltpu.VMEM((UNITS, 32, 16, WIDE), BF16),
            pltpu.VMEM((512, 256), F32),
            pltpu.VMEM((64, 128), F32),
            pltpu.VMEM((7, 8, 128), F32),
            dma((7,)),
            dma((3, 8)),
            dma((3, 8)),
            dma((3, 8)),
            dma((3, 8)),
            dma,
            dma((GROUPS,)),
            dma((UNITS,)),
            dma((UNITS, 20)),
            dma,
            dma((4, GROUPS)),
            dma,
            dma((4, GROUPS)),
            dma((7,)),
            dma((7,)),
        ],
        compiler_params=pltpu.CompilerParams(
            collective_id=0, has_side_effects=True, vmem_limit_bytes=63 * 1024 * 1024
        ),
        cost_estimate=pl.CostEstimate(flops=4 * 10**9, bytes_accessed=10**7, transcendentals=0),
    )(
        query_grads.reshape(160, 1280),
        in_inverse,
        out_inverse,
        activations.reshape(GROUPS, 2, 32, 1280),
        errors,
    )


def solution(mesh):
    return jax.shard_map(
        per_device,
        mesh=mesh,
        in_specs=(P("dp", "param", None), P(), P(), P("dp", "param", None), P("dp", None, "param")),
        out_specs=P(("dp", "param"), None),
        check_vma=False,
    )
```
